512 devices in a mesh: dp: 16 (over x, z_hi), seq: 32 (over z_lo, y, core).
Axes of the slice: x: 4, y: 4, z: 16 (z_hi: 4, z_lo: 4; z = z_hi * 4 + z_lo), core: 2. Of those that a mesh axis runs over, the one named last changes fastest.
Arguments:
- queries: bfloat16 [16, 4096, 4096], P('dp', 'seq'), may hold values from -6 to 6
- key_rows: bfloat16 [16, 4096, 512], P('dp', 'seq'), may hold values from -6 to 6
- value_rows: bfloat16 [16, 4096, 512], P('dp', 'seq'), may hold values from -6 to 6
- out_grad: bfloat16 [16, 4096, 4096], P('dp', 'seq'), may hold values from -0.59765625 to 0.59765625
- log_norm: float32 [16, 4096, 32], P('dp', 'seq'), may hold values from 2 to 7
- row_delta: float32 [16, 4096, 32], P('dp', 'seq'), may hold values from -5 to 5
- doc_ids: int32 [16, 4096], P('dp', 'seq'), may hold values from 0 to 15, as said below
Outputs:
- query_grad: bfloat16 [16, 4096, 4096], P('dp', 'seq')
- key_grad: bfloat16 [16, 4096, 512], P('dp', 'seq')
- value_grad: bfloat16 [16, 4096, 512], P('dp', 'seq')
The draws below stay inside these ranges and needn't reach their ends.
Inputs may be any that keep to these rules, and one draw needn't show every extreme that they name: `doc_ids`: in each sequence document numbers never fall and all 16 numbers occur. The sequence that stands p-th in an order drawn from the seed (p from 0) has a bound b = 4096 / 2 ** (1 + p % 4) on its documents' lengths, and one of its documents has exactly b tokens; so some sequence always holds a document of 2048 tokens, and where b = 256 every document has b tokens.
All inputs are finite; a program needn't handle non-finite values.
Results may differ from the reference program's by a relative error of at most 0.0026.
The reference program's roundings to bfloat16 on the way count: a program that leaves them out, or rounds other values in their place, can miss the bound.
Values may be sent and summed in bfloat16 or wider, within the bound.
A program may use at most 64 MiB of HBM per device.

```python
import jax
import jax.numpy as jnp
from jax import lax

QH = 32
KVH = 4
HDIM = 128
DOCS = 16
NSEQ = 16
SEQLEN = 4096


def one_sequence(seq_key, level):
    length_key, shuffle_key, place_key = jax.random.split(seq_key, 3)
    others = DOCS - 1
    pairs = others // 2
    multiples = jnp.array([1, 2, 4, 8], jnp.int32)
    bound = SEQLEN // 16 * multiples[level]
    remaining = SEQLEN - bound
    share = remaining // others
    leftover = remaining % others
    order_ids = jnp.arange(others, dtype=jnp.int32)
    lengths = share + (order_ids < leftover).astype(jnp.int32)
    margin = jnp.maximum(jnp.minimum(share - 1, bound - share - 2), 0)
    raw = jax.random.randint(length_key, (pairs,), 0, 1 << 20, dtype=jnp.int32)
    shift_by = raw % (2 * margin + 1) - margin
    lengths = lengths.at[0:2 * pairs:2].add(shift_by)
    lengths = lengths.at[1:2 * pairs:2].add(-shift_by)
    shuffled = jax.random.permutation(shuffle_key, others).astype(jnp.int32)
    lengths = lengths[shuffled]
    place = jax.random.randint(place_key, (), 0, DOCS, dtype=jnp.int32)
    slots = jnp.arange(DOCS, dtype=jnp.int32)
    source = jnp.clip(slots - (slots > place).astype(jnp.int32), 0, others - 1)
    full = jnp.where(slots == place, bound, lengths[source])
    ends = jnp.cumsum(full).astype(jnp.int32)
    tokens = jnp.arange(SEQLEN, dtype=jnp.int32)
    return jnp.sum((tokens[:, None] >= ends[None, :]).astype(jnp.int32), axis=1).astype(jnp.int32)


def draw_doc_ids(key, part):
    key = jax.random.fold_in(key, 7)
    order_key, seq_key = jax.random.split(key)
    order = jax.random.permutation(order_key, NSEQ).astype(jnp.int32)
    levels = 3 - order % 4
    seq_keys = jax.random.split(seq_key, NSEQ)
    return jax.vmap(one_sequence)(seq_keys, levels).astype(jnp.int32)


def steps_of(rng, extent, cuts, least, largest):
    level = 1.0
    for axis_at, parts in cuts:
        steps = jax.random.uniform(jax.random.fold_in(jax.random.fold_in(rng, 6), axis_at), (parts,), jnp.float32, least / len(cuts), largest / len(cuts))
        level = level * jnp.repeat(jnp.exp(steps), extent[axis_at] // parts).reshape((-1,) + (1,) * (len(extent) - 1 - axis_at))
    return level


def noise(rng, shape, scale, most, shards=(), held_as=jnp.bfloat16):
    entries = scale * jax.random.normal(rng, shape, jnp.float32)
    if shards:
        entries = entries * steps_of(rng, shape, shards, -0.22, 0.18)
    return jnp.clip(entries, -most, most).astype(held_as)


def setup_inputs(seed: int = 0) -> dict:
    splits = jax.random.split(jax.random.key(seed), 8)
    return {
        "queries": noise(splits[0], (NSEQ, SEQLEN, QH * HDIM), 1.0, 6.0, ((0, 16), (1, 32))),
        "key_rows": noise(splits[1], (NSEQ, SEQLEN, KVH * HDIM), 1.0, 6.0, ((0, 16), (1, 32))),
        "value_rows": noise(splits[2], (NSEQ, SEQLEN, KVH * HDIM), 1.0, 6.0, ((0, 16), (1, 32))),
        "out_grad": noise(splits[3], (NSEQ, SEQLEN, QH * HDIM), 0.1, 0.59765625, ((0, 16), (1, 32))),
        "log_norm": jnp.clip(2.0 + 5.0 * jax.random.uniform(splits[4], (NSEQ, SEQLEN, QH), jnp.float32) ** steps_of(splits[4], (NSEQ, SEQLEN, QH), ((0, 16), (1, 32)), -0.2, 0.2), 2.0, 7.0),
        "row_delta": noise(splits[5], (NSEQ, SEQLEN, QH), 1.0, 5.0, ((0, 16), (1, 32)), jnp.float32),
        "doc_ids": draw_doc_ids(jax.random.fold_in(splits[7], 71), 0),
    }


def group_grads(queries, key_rows, value_rows, out_grad, log_norm, row_delta, doc_ids, item):
    group = QH // KVH
    softmax_scale = HDIM ** -0.5
    seq_index = item // KVH
    kv_head = item % KVH
    q_seq = lax.dynamic_index_in_dim(queries, seq_index, 0, keepdims=False).astype(jnp.float32).reshape(SEQLEN, QH, HDIM)
    g_seq = lax.dynamic_index_in_dim(out_grad, seq_index, 0, keepdims=False).astype(jnp.float32).reshape(SEQLEN, QH, HDIM)
    k_seq = lax.dynamic_index_in_dim(key_rows, seq_index, 0, keepdims=False).astype(jnp.float32).reshape(SEQLEN, KVH, HDIM)
    v_seq = lax.dynamic_index_in_dim(value_rows, seq_index, 0, keepdims=False).astype(jnp.float32).reshape(SEQLEN, KVH, HDIM)
    key_head = lax.dynamic_index_in_dim(k_seq, kv_head, 1, keepdims=False)
    value_head = lax.dynamic_index_in_dim(v_seq, kv_head, 1, keepdims=False)
    lse_seq = lax.dynamic_index_in_dim(log_norm, seq_index, 0, keepdims=False)
    delta_seq = lax.dynamic_index_in_dim(row_delta, seq_index, 0, keepdims=False)
    docs = lax.dynamic_index_in_dim(doc_ids, seq_index, 0, keepdims=False)
    positions = jnp.arange(SEQLEN, dtype=jnp.int32)
    key_mask = (docs[:, None] == docs[None, :]) & (positions[None, :] <= positions[:, None])

    def one_head(state_now, offset):
        key_acc, value_acc = state_now
        head = (kv_head * group + offset).astype(jnp.int32)
        q_head = lax.dynamic_index_in_dim(q_seq, head, 1, keepdims=False)
        g_head = lax.dynamic_index_in_dim(g_seq, head, 1, keepdims=False)
        lse_head = lax.dynamic_index_in_dim(lse_seq, head, 1, keepdims=False)
        delta_head = lax.dynamic_index_in_dim(delta_seq, head, 1, keepdims=False)
        scores = softmax_scale * jnp.dot(q_head, key_head.T, precision=lax.Precision.HIGHEST, preferred_element_type=jnp.float32)
        attn_prob = jnp.where(key_mask, jnp.exp(scores - lse_head[:, None]), 0.0)
        prob_grad = jnp.dot(g_head, value_head.T, precision=lax.Precision.HIGHEST, preferred_element_type=jnp.float32)
        score_grad = attn_prob * (prob_grad - delta_head[:, None])
        prob_half = lax.optimization_barrier(attn_prob.astype(jnp.bfloat16)).astype(jnp.float32)
        score_half = lax.optimization_barrier(score_grad.astype(jnp.bfloat16)).astype(jnp.float32)
        value_acc = value_acc + jnp.dot(prob_half.T, g_head, precision=lax.Precision.HIGHEST, preferred_element_type=jnp.float32)
        key_acc = key_acc + jnp.dot(score_half.T, q_head, precision=lax.Precision.HIGHEST, preferred_element_type=jnp.float32)
        query_part = softmax_scale * jnp.dot(score_half, key_head, precision=lax.Precision.HIGHEST, preferred_element_type=jnp.float32)
        return (key_acc, value_acc), query_part.astype(jnp.bfloat16)

    empty = jnp.zeros((SEQLEN, HDIM), jnp.float32)
    (key_acc, value_acc), query_parts = lax.scan(one_head, (empty, empty), jnp.arange(group, dtype=jnp.int32))
    return query_parts, (softmax_scale * key_acc).astype(jnp.bfloat16), value_acc.astype(jnp.bfloat16)


def reference(queries, key_rows, value_rows, out_grad, log_norm, row_delta, doc_ids):
    items = jnp.arange(NSEQ * KVH, dtype=jnp.int32)

    def run_item(item):
        return group_grads(queries, key_rows, value_rows, out_grad, log_norm, row_delta, doc_ids, item)

    query_parts, key_parts, value_parts = lax.map(run_item, items)
    query_grad = query_parts.reshape(NSEQ, QH, SEQLEN, HDIM).transpose(0, 2, 1, 3).reshape(NSEQ, SEQLEN, QH * HDIM)
    key_grad = key_parts.reshape(NSEQ, KVH, SEQLEN, HDIM).transpose(0, 2, 1, 3).reshape(NSEQ, SEQLEN, KVH * HDIM)
    value_grad = value_parts.reshape(NSEQ, KVH, SEQLEN, HDIM).transpose(0, 2, 1, 3).reshape(NSEQ, SEQLEN, KVH * HDIM)
    return (query_grad, key_grad, value_grad)
```

```python
import jax
import jax.numpy as jnp
from jax import lax
from jax.experimental import pallas as pl
from jax.experimental.pallas import tpu as pltpu
from jax.sharding import PartitionSpec as P

F32, BF16 = jnp.float32, jnp.bfloat16
HDIM = 128
TOK = 128
BLK = 2 * TOK
HEADS = 16
GROUP = 8
ROWS = GROUP * BLK
QC = 512
EXTRA = 16
NCH = 4
CH = BLK // NCH
SCALE = HDIM**-0.5
EXP_SCALE = SCALE * 1.4426950408889634
FAR = -1e30
ITEMS = ("k", "v", "doc", "lse", "delta", "q", "g")


def dot(a, b):
    return jnp.dot(a, b, preferred_element_type=F32)


def split3(x):
    hi = x.astype(BF16).astype(F32)
    mid = (x - hi).astype(BF16).astype(F32)
    return hi, mid, x - hi - mid


def kernel(
    q_in, k_in, v_in, g_in, lse_in, delta_in, doc_in,
    dq_out, dk_out, dv_out,
    kv, part_out, part_in, acc, zin, q_buf, g_buf, qt, gt, dqt, dq_half, fin, lse_buf, delta_buf, doc_buf,
    local_sem, x_send, x_recv, kv_send, kv_recv, kvz_send, p_send, p_recv, z_send, z_recv, f_send, f_recv, f_local,
):
    me = lax.axis_index("seq")
    core = me % 2
    y = (me // 2) % 4
    z = me // 8
    other = 1 - core

    def device(zz, yy, cc):
        return {"seq": (zz * 4 + yy) * 2 + cc}

    def remote(src, dst, send, recv, to):
        return pltpu.make_async_remote_copy(
            src_ref=src, dst_ref=dst, send_sem=send, recv_sem=recv, device_id=to, device_id_type=pl.DeviceIdType.MESH
        )

    sibling = device(z, y, other)
    down, up = device(z - 1, y, core), device(z + 1, y, core)

    def part_of(name, half):
        wide = pl.ds(pl.multiple_of(half * HEADS * HDIM, HEADS * HDIM), HEADS * HDIM)
        narrow = pl.ds(pl.multiple_of(half * 2 * HDIM, 2 * HDIM), 2 * HDIM)
        return {
            "q": lambda: q_in.at[:, wide],
            "g": lambda: g_in.at[:, wide],
            "k": lambda: k_in.at[:, narrow],
            "v": lambda: v_in.at[:, narrow],
            "lse": lambda: lse_in,
            "delta": lambda: delta_in,
            "doc": lambda: doc_in,
        }[name]()

    def place_of(name):
        rows = pl.ds(pl.multiple_of(core * TOK, TOK), TOK)
        return {
            "q": lambda: q_buf.at[rows],
            "g": lambda: g_buf.at[rows],
            "k": lambda: kv.at[0, y, rows, pl.ds(0, 2 * HDIM)],
            "v": lambda: kv.at[0, y, rows, pl.ds(2 * HDIM, 2 * HDIM)],
            "lse": lambda: lse_buf.at[rows],
            "delta": lambda: delta_buf.at[rows],
            "doc": lambda: doc_buf.at[core],
        }[name]()

    def local(name):
        return pltpu.make_async_copy(part_of(name, core), place_of(name), local_sem.at[ITEMS.index(name)])

    def swap(name):
        i = ITEMS.index(name)
        return remote(part_of(name, other), place_of(name), x_send.at[i], x_recv.at[i], sibling)

    for name in ITEMS:
        local(name).start()

    barrier = pltpu.get_barrier_semaphore()

    def greet(to):
        pl.semaphore_signal(barrier, inc=1, device_id=to, device_id_type=pl.DeviceIdType.MESH)

    greet(sibling)
    for apart in range(1, 4):
        greet(device(z, (y + apart) % 4, core))
    pl.when(z > 0)(lambda: greet(down))
    pl.when(z < 3)(lambda: greet(up))
    pl.semaphore_wait(barrier, 4 + (z + 3) // 4 + (6 - z) // 4)

    for name in ITEMS:
        swap(name).start()

    def arrive(name):
        local(name).wait()
        swap(name).wait_recv()

    def along_z(dz):
        return remote(kv.at[dz, y], kv.at[dz + 1, y], kvz_send.at[dz], kv_recv.at[dz + 1, y], up)

    def along_y(dz, to):
        return remote(kv.at[dz, y], kv.at[dz, y], kv_send.at[dz, to], kv_recv.at[dz, y], device(z, to, core))

    def arrived(dz, yk):
        remote(kv.at[dz, yk], kv.at[dz, yk], kv_send.at[dz, yk], kv_recv.at[dz, yk], sibling).wait_recv()

    def each_target(dz, act):
        for apart in range(1, 4):
            to = (y + apart) % 4
            if dz == 0:
                pl.when(to > y)(lambda to=to: act(to))
            elif dz == 1:
                act(to)
            else:
                pl.when(to < y)(lambda to=to: act(to))

    for name in ("k", "v", "doc"):
        arrive(name)
    docs = jnp.concatenate([doc_buf[0], doc_buf[1]], axis=1).astype(F32)
    docs16 = jnp.broadcast_to(docs, (EXTRA, BLK))
    kv[0, y, pl.ds(BLK, EXTRA), pl.ds(0, BLK)] = docs16.astype(BF16)
    kv[0, y, pl.ds(BLK, EXTRA), pl.ds(BLK, BLK)] = jnp.zeros((EXTRA, BLK), BF16)
    pl.when(z < 3)(lambda: along_z(0).start())
    each_target(0, lambda to: along_y(0, to).start())

    for name in ("lse", "delta", "q", "g"):
        arrive(name)
    sixteen = lax.broadcasted_iota(jnp.int32, (EXTRA, BLK), 0)
    bias = jnp.where(docs16 == sixteen.astype(F32), 0.0, FAR).astype(BF16)
    blank = jnp.zeros((EXTRA, BLK), BF16)
    zeros = jnp.zeros((HDIM - 2 * EXTRA, BLK), BF16)
    lse_t = jnp.where(core == 0, lse_buf[:, pl.ds(0, HEADS)], lse_buf[:, pl.ds(HEADS, HEADS)]).T
    delta_t = jnp.where(core == 0, delta_buf[:, pl.ds(0, HEADS)], delta_buf[:, pl.ds(HEADS, HEADS)]).T
    lse_parts = split3(lse_t * (-1.0 / SCALE))
    delta_parts = split3(-delta_t)
    for head in range(HEADS):
        h, cols = head // GROUP, pl.ds(head % GROUP * BLK, BLK)
        lanes = pl.ds(head * HDIM, HDIM)
        for source, out, first, top, parts in (
            (q_buf, qt, 0, bias, lse_parts), (g_buf, gt, 3, blank, delta_parts)
        ):
            rows = jnp.zeros((EXTRA, BLK), F32)
            for i, part in enumerate(parts):
                rows = jnp.where(sixteen == first + i, jnp.broadcast_to(part[head : head + 1], (EXTRA, BLK)), rows)
            out[h, pl.ds(0, HDIM), cols] = source[:, lanes].T
            out[h, pl.ds(HDIM, EXTRA), cols] = top
            out[h, pl.ds(HDIM + EXTRA, EXTRA), cols] = rows.astype(BF16)
            out[h, pl.ds(HDIM + 2 * EXTRA, HDIM - 2 * EXTRA), cols] = zeros

    def return_y(dz, to):
        return remote(
            part_out.at[dz, to], part_in.at[dz, y], p_send.at[dz, to], p_recv.at[dz, y], device(z, to, core)
        )

    def work(dz, yk, own):
        marks = (kv[dz, yk, pl.ds(BLK, EXTRA), pl.ds(0, BLK)].astype(F32) == sixteen.astype(F32)).astype(F32)
        ones = (lax.broadcasted_iota(jnp.int32, (HDIM - EXTRA, BLK), 0) < 6).astype(F32)
        tail = jnp.concatenate([marks, ones], axis=0).T.astype(BF16)
        for h in range(2):
            keys = kv[dz, yk, pl.ds(0, BLK), pl.ds(h * HDIM, HDIM)]
            values = kv[dz, yk, pl.ds(0, BLK), pl.ds((2 + h) * HDIM, HDIM)]
            keys_t = keys.T
            keys_long = jnp.concatenate([keys, tail], axis=1)
            values_long = jnp.concatenate([values, tail], axis=1)
            dk = jnp.zeros((BLK, HDIM), F32)
            dv = jnp.zeros((BLK, HDIM), F32)
            for c in range(ROWS // QC):
                cols = pl.ds(c * QC, QC)
                heads = [h * GROUP + c * (QC // BLK) + i for i in range(QC // BLK)]
                q_rows = jnp.concatenate([q_buf[:, pl.ds(n * HDIM, HDIM)] for n in heads], axis=0)
                g_rows = jnp.concatenate([g_buf[:, pl.ds(n * HDIM, HDIM)] for n in heads], axis=0)
                prob = jnp.exp2(dot(keys_long, qt[h, :, cols]) * EXP_SCALE)
                if own:
                    k_pos = lax.broadcasted_iota(jnp.int32, (BLK, QC), 0)
                    q_pos = lax.broadcasted_iota(jnp.int32, (BLK, QC), 1) % BLK
                    prob = jnp.where(k_pos <= q_pos, prob, 0.0)
                grad = prob * dot(values_long, gt[h, :, cols])
                prob_half = prob.astype(BF16)
                grad_half = grad.astype(BF16)
                dv = dv + dot(prob_half, g_rows)
                dk = dk + dot(grad_half, q_rows)
                if own:
                    dqt[h, :, cols] = dot(keys_t, grad_half)
                else:
                    dqt[h, :, cols] += dot(keys_t, grad_half)
            dk_lanes, dv_lanes = pl.ds(h * HDIM, HDIM), pl.ds((2 + h) * HDIM, HDIM)
            if own:
                acc[0, :, dk_lanes] = dk
                acc[0, :, dv_lanes] = dv
            else:

                @pl.when(yk == y)
                def _():
                    acc[dz, :, dk_lanes] = dk
                    acc[dz, :, dv_lanes] = dv

                @pl.when(yk != y)
                def _():
                    part_out[dz, yk, :, dk_lanes] = dk.astype(BF16)
                    part_out[dz, yk, :, dv_lanes] = dv.astype(BF16)

    work(0, y, True)

    @pl.loop(1, 4)
    def _(turn):
        dz = turn % 3
        first = (2 - dz) // 2 * (4 - y)
        last = 4 - dz // 2 * y
        live = (z - dz + 4) // 4

        @pl.loop(first, first + live * (last - first))
        def _(i):
            yk = (y + i) % 4
            pl.when((dz != 2) | (i != 0))(lambda: arrived(dz, yk))

            @pl.when((dz == 1) & (i == 0))
            def _():
                pl.when(z < 3)(lambda: along_z(1).start())
                each_target(1, lambda to: along_y(1, to).start())

            work(dz, yk, False)

            @pl.when((dz == 1) & (i == 0) & (z > 1))
            def _():
                arrived(2, y)
                each_target(2, lambda to: along_y(2, to).start())

            pl.when(yk != y)(lambda: return_y(dz, yk).start())

    for head in range(HEADS):
        h, cols = head // GROUP, pl.ds(head % GROUP * BLK, BLK)
        dq_half[:, pl.ds(head * HDIM, HDIM)] = (dqt[h, :, cols].T * SCALE).astype(BF16)
    mine = pl.ds(pl.multiple_of(core * TOK, TOK), TOK)
    theirs = pl.ds(pl.multiple_of(other * TOK, TOK), TOK)
    wide = pl.ds(pl.multiple_of(core * HEADS * HDIM, HEADS * HDIM), HEADS * HDIM)
    narrow = pl.ds(pl.multiple_of(core * 2 * HDIM, 2 * HDIM), 2 * HDIM)
    results = (
        (lambda rows: dq_half.at[rows], lambda: dq_out.at[:, wide]),
        (lambda rows: fin.at[rows, pl.ds(0, 2 * HDIM)], lambda: dk_out.at[:, narrow]),
        (lambda rows: fin.at[rows, pl.ds(2 * HDIM, 2 * HDIM)], lambda: dv_out.at[:, narrow]),
    )

    def keep(i):
        return pltpu.make_async_copy(results[i][0](mine), results[i][1](), f_local.at[i])

    def give(i):
        return remote(results[i][0](theirs), results[i][1](), f_send.at[i], f_recv.at[i], sibling)

    keep(0).start()
    give(0).start()

    def take(dz, yk):
        remote(
            part_out.at[dz, yk], part_in.at[dz, yk], p_send.at[dz, yk], p_recv.at[dz, yk], sibling
        ).wait_recv()
        acc[dz] += part_in[dz, yk].astype(F32)

    def each_source(dz, act):
        each_target(dz, act)

    def piece(dz, c):
        rows = pl.ds(c * CH, CH)
        return remote(acc.at[dz, rows], zin.at[2 - dz, rows], z_send.at[2 - dz, c], z_recv.at[2 - dz, c], down)

    def join(dz, c):
        rows = pl.ds(c * CH, CH)
        remote(acc.at[dz, rows], zin.at[1 - dz, rows], z_send.at[1 - dz, c], z_recv.at[1 - dz, c], sibling).wait_recv()
        acc[dz, rows] += zin[1 - dz, rows]

    @pl.when(z > 1)
    def _():
        each_source(2, lambda yk: take(2, yk))
        for c in range(NCH):
            piece(2, c).start()

    @pl.when(z > 0)
    def _():
        each_source(1, lambda yk: take(1, yk))
        for c in range(NCH):
            pl.when(z < 3)(lambda: join(1, c))
            piece(1, c).start()

    each_source(0, lambda yk: take(0, yk))
    for c in range(NCH):
        rows = pl.ds(c * CH, CH)
        pl.when(z < 3)(lambda: join(0, c))
        fin[rows, pl.ds(0, 2 * HDIM)] = (acc[0, rows, pl.ds(0, 2 * HDIM)] * SCALE).astype(BF16)
        fin[rows, pl.ds(2 * HDIM, 2 * HDIM)] = acc[0, rows, pl.ds(2 * HDIM, 2 * HDIM)].astype(BF16)
    for i in (1, 2):
        keep(i).start()
        give(i).start()

    for name in ITEMS:
        swap(name).wait_send()
    pl.when(z < 3)(lambda: along_z(0).wait_send())
    pl.when((z > 0) & (z < 3))(lambda: along_z(1).wait_send())
    each_target(0, lambda to: along_y(0, to).wait_send())
    pl.when(z > 0)(lambda: each_target(1, lambda to: along_y(1, to).wait_send()))
    pl.when(z > 1)(lambda: each_target(2, lambda to: along_y(2, to).wait_send()))
    for apart in range(1, 4):
        to = (y + apart) % 4
        pl.when(to < y)(lambda: return_y(0, to).wait_send())
        pl.when(z > 0)(lambda: return_y(1, to).wait_send())
        pl.when((z > 1) & (to > y))(lambda: return_y(2, to).wait_send())
    for c in range(NCH):
        pl.when(z > 1)(lambda: piece(2, c).wait_send())
        pl.when(z > 0)(lambda: piece(1, c).wait_send())
    for i in range(3):
        keep(i).wait()
        give(i).wait()


def on_device(queries, key_rows, value_rows, out_grad, log_norm, row_delta, doc_ids):
    dma = pltpu.SemaphoreType.DMA
    items = len(ITEMS)
    dq, dk, dv = pl.pallas_call(
        kernel,
        out_shape=(
            jax.ShapeDtypeStruct((TOK, 2 * HEADS * HDIM), BF16),
            jax.ShapeDtypeStruct((TOK, 4 * HDIM), BF16),
            jax.ShapeDtypeStruct((TOK, 4 * HDIM), BF16),
        ),
        in_specs=[pl.BlockSpec(memory_space=pl.ANY)] * 7,
        out_specs=[pl.BlockSpec(memory_space=pl.ANY)] * 3,
        scratch_shapes=[
            pltpu.VMEM((3, 4, BLK + EXTRA, 4 * HDIM), BF16),
            pltpu.VMEM((3, 4, BLK, 4 * HDIM), BF16),
            pltpu.VMEM((3, 4, BLK, 4 * HDIM), BF16),
            pltpu.VMEM((3, BLK, 4 * HDIM), F32),
            pltpu.VMEM((2, BLK, 4 * HDIM), F32),
            pltpu.VMEM((BLK, HEADS * HDIM), BF16),
            pltpu.VMEM((BLK, HEADS * HDIM), BF16),
            pltpu.VMEM((2, 2 * HDIM, ROWS), BF16),
            pltpu.VMEM((2, 2 * HDIM, ROWS), BF16),
            pltpu.VMEM((2, HDIM, ROWS), F32),
            pltpu.VMEM((BLK, HEADS * HDIM), BF16),
            pltpu.VMEM((BLK, 4 * HDIM), BF16),
            pltpu.VMEM((BLK, 2 * HEADS), F32),
            pltpu.VMEM((BLK, 2 * HEADS), F32),
            pltpu.VMEM((2, 1, TOK), jnp.int32),
            dma((items,)),
            dma((items,)),
            dma((items,)),
            dma((3, 4)),
            dma((3, 4)),
            dma((2,)),
            dma((3, 4)),
            dma((3, 4)),
            dma((2, NCH)),
            dma((2, NCH)),
            dma((3,)),
            dma((3,)),
            dma((3,)),
        ],
        compiler_params=pltpu.CompilerParams(
            collective_id=0, has_side_effects=True, vmem_limit_bytes=48 * 2**20
        ),
        name="attention_backward",
    )(queries[0], key_rows[0], value_rows[0], out_grad[0], log_norm[0], row_delta[0], doc_ids)
    return dq[None], dk[None], dv[None]


def solution(mesh):
    return jax.shard_map(
        on_device,
        mesh=mesh,
        in_specs=(P("dp", "seq", None),) * 6 + (P("dp", "seq"),),
        out_specs=(P("dp", "seq", None),) * 3,
        check_vma=False,
    )
```

```python
import jax
import jax.numpy as jnp
from jax import lax
from jax.experimental import pallas as pl
from jax.experimental.pallas import tpu as pltpu
from jax.sharding import PartitionSpec as P

F32, BF16 = jnp.float32, jnp.bfloat16
HDIM = 128
TOK = 128
BLK = 2 * TOK
HEADS = 4
GROUP = 8
WIDE = HEADS * HDIM
COLS = HEADS * BLK
QC = 1024
SCALE = HDIM**-0.5
EXP_SCALE = SCALE * 1.4426950408889634
FAR = -1e30
MARKS = 16
KINDS = ("q", "g", "lse", "delta", "doc")
SUMS = BF16


def dot(a, b):
    return jnp.dot(a, b, preferred_element_type=F32)


def split3(x):
    hi = x.astype(BF16).astype(F32)
    mid = (x - hi).astype(BF16).astype(F32)
    return hi, mid, x - hi - mid


def kernel(
    q_in, k_in, v_in, g_in, lse_in, delta_in, doc_in,
    dq_out, dk_out, dv_out,
    q_buf, g_buf, lse_buf, delta_buf, doc_buf, kv, qt, gt, dqt, tails, keys_t, acc, xin, zout, zin, dq_half, fin,
    x_local, x_send, x_recv, kv_local, kv_send, kv_recv, half_send, half_recv, kvz_send, kvz_recv, docz_send, docz_recv,
    s_send, s_recv, z_send, z_recv, dq_local, dq_send, dq_recv, f_local, f_send, f_recv,
):
    me = lax.axis_index("seq")
    core = me % 2
    other = 1 - core
    y = (me // 2) % 4
    z = me // 8
    here = me % 8

    def remote(src, dst, send, recv, to):
        return pltpu.make_async_remote_copy(
            src_ref=src, dst_ref=dst, send_sem=send, recv_sem=recv,
            device_id={"seq": to}, device_id_type=pl.DeviceIdType.MESH,
        )

    row = z * 8
    sibling = row + y * 2 + other
    down, up = me - 8, me + 8

    def lanes(i, size):
        return pl.ds(pl.multiple_of(i * size, size), size)

    def source(kind, p):
        return {
            "q": lambda: q_in.at[:, lanes(p, WIDE)],
            "g": lambda: g_in.at[:, lanes(p, WIDE)],
            "lse": lambda: lse_in.at[lanes(p // 2, GROUP)],
            "delta": lambda: delta_in.at[lanes(p // 2, GROUP)],
            "doc": lambda: doc_in,
        }[kind]()

    def target(kind, p):
        return {
            "q": lambda: q_buf.at[p],
            "g": lambda: g_buf.at[p],
            "lse": lambda: lse_buf.at[p],
            "delta": lambda: delta_buf.at[p],
            "doc": lambda: doc_buf.at[0, p],
        }[kind]()

    def stay(kind):
        return pltpu.make_async_copy(source(kind, here), target(kind, here), x_local.at[KINDS.index(kind)])

    def send(kind, p):
        i = KINDS.index(kind)
        return remote(source(kind, p), target(kind, here), x_send.at[i, p], x_recv.at[i, here], row + p)

    def receive(kind, p):
        i = KINDS.index(kind)
        remote(source(kind, p), target(kind, p), x_send.at[i, p], x_recv.at[i, p], sibling).wait_recv()

    def kv_place(part, column):
        return kv.at[0, core, column, :, pl.ds(part * HDIM, HDIM)]

    def kv_source(part, column):
        return (k_in, v_in)[part].at[:, lanes(column, HDIM)]

    def kv_stay(part):
        return pltpu.make_async_copy(kv_source(part, y), kv_place(part, y), kv_local.at[part])

    def kv_give(part, column):
        return remote(
            kv_source(part, column), kv_place(part, y), kv_send.at[part, column], kv_recv.at[part, y],
            row + column * 2 + core,
        )

    def kv_take(part, column):
        remote(
            kv_source(part, column), kv_place(part, column), kv_send.at[part, column], kv_recv.at[part, column], sibling
        ).wait_recv()

    for part in range(2):
        kv_stay(part).start()
    for kind in KINDS:
        stay(kind).start()

    barrier = pltpu.get_barrier_semaphore()

    def greet(to):
        pl.semaphore_signal(barrier, inc=1, device_id={"seq": to}, device_id_type=pl.DeviceIdType.MESH)

    for apart in range(1, 8):
        greet(row + (here + apart) % 8)
    pl.when(z > 0)(lambda: greet(down))
    pl.when(z < 3)(lambda: greet(up))
    pl.semaphore_wait(barrier, 7 + (z + 3) // 4 + (6 - z) // 4)

    columns = [(y + apart) % 4 for apart in (1, 3, 2)]
    others = [sibling - row] + [column * 2 + c for column in columns for c in range(2)]
    for column in columns:
        for part in range(2):
            kv_give(part, column).start()
    for p in others:
        send("doc", p).start()
    for kind in ("q", "g", "lse", "delta"):
        send(kind, others[0]).start()

    def half(dz):
        return remote(kv.at[dz, core], kv.at[dz, core], half_send.at[dz], half_recv.at[dz], sibling)

    def half_take(dz):
        remote(kv.at[dz, other], kv.at[dz, other], half_send.at[dz], half_recv.at[dz], sibling).wait_recv()

    def kv_up(dz):
        return remote(kv.at[dz, core], kv.at[dz + 1, core], kvz_send.at[dz], kvz_recv.at[dz], up)

    def doc_up(dz):
        return remote(doc_buf.at[dz], doc_buf.at[dz + 1], docz_send.at[dz], docz_recv.at[dz], up)

    for part in range(2):
        kv_stay(part).wait()
        for column in columns:
            kv_take(part, column)
    half(0).start()
    pl.when(z < 3)(lambda: kv_up(0).start())
    for p in others[1:5]:
        for kind in ("q", "g", "lse", "delta"):
            send(kind, p).start()
    stay("doc").wait()
    for p in others:
        receive("doc", p)
    pl.when(z < 3)(lambda: doc_up(0).start())
    acc[...] = jnp.zeros_like(acc)
    half_take(0)

    sixteen = lax.broadcasted_iota(jnp.int32, (MARKS, BLK), 0).astype(F32)

    def marks_of(dz, column):
        docs = jnp.concatenate([doc_buf[dz, column * 2], doc_buf[dz, column * 2 + 1]], axis=1).astype(F32)
        return jnp.broadcast_to(docs, (MARKS, BLK)) == sixteen

    def prepare_keys(dz):
        @pl.loop(0, 4)
        def _(column):
            marks = marks_of(dz, column).astype(F32)
            ones = (lax.broadcasted_iota(jnp.int32, (HDIM - MARKS, BLK), 0) < 6).astype(F32)
            tails[dz, column] = jnp.concatenate([marks, ones], axis=0).T.astype(BF16)
            keys_t[dz, column] = both(kv, dz, column, 0).T

    def both(ref, dz, column, part):
        at = pl.ds(part * HDIM, HDIM)
        return jnp.concatenate([ref[dz, 0, column, :, at], ref[dz, 1, column, :, at]], axis=0)

    def rows_of(buf, column, head):
        at = pl.ds(head * HDIM, HDIM)
        return jnp.concatenate([buf[column * 2, :, at], buf[column * 2 + 1, :, at]], axis=0)

    def prepare_queries(column):
        bias = jnp.where(marks_of(0, column), 0.0, FAR).astype(BF16)
        blank = jnp.zeros((MARKS, BLK), BF16)
        zeros = jnp.zeros((HDIM - 2 * MARKS, BLK), BF16)

        def statistic(buf, factor):
            pair = [buf[column * 2], buf[column * 2 + 1]]
            pair = [jnp.where(core == 0, rows[:HEADS], rows[HEADS:]) for rows in pair]
            return split3(jnp.concatenate(pair, axis=1) * factor)

        for buf, out, first, top, parts in (
            (q_buf, qt, 0, bias, statistic(lse_buf, -1.0 / SCALE)), (g_buf, gt, 3, blank, statistic(delta_buf, -1.0))
        ):
            for head in range(HEADS):
                at = pl.ds(head * BLK, BLK)
                rows = jnp.zeros((MARKS, BLK), F32)
                for i, part in enumerate(parts):
                    rows = jnp.where(sixteen == first + i, jnp.broadcast_to(part[head : head + 1], (MARKS, BLK)), rows)
                out[column, pl.ds(0, HDIM), at] = rows_of(buf, column, head).T
                out[column, pl.ds(HDIM, MARKS), at] = top
                out[column, pl.ds(HDIM + MARKS, MARKS), at] = rows.astype(BF16)
                out[column, pl.ds(HDIM + 2 * MARKS, HDIM - 2 * MARKS), at] = zeros
        dqt[column] = jnp.zeros((HDIM, COLS), F32)

    def work(dz, yk, yq, own):
        tail = tails[dz, yk]
        keys_long = jnp.concatenate([both(kv, dz, yk, 0), tail], axis=1)
        values_long = jnp.concatenate([both(kv, dz, yk, 1), tail], axis=1)
        dk = jnp.zeros((BLK, HDIM), F32)
        dv = jnp.zeros((BLK, HDIM), F32)
        for c in range(COLS // QC):
            cols = pl.ds(c * QC, QC)
            heads = [c * (QC // BLK) + i for i in range(QC // BLK)]
            q_rows = jnp.concatenate([rows_of(q_buf, yq, n) for n in heads], axis=0)
            g_rows = jnp.concatenate([rows_of(g_buf, yq, n) for n in heads], axis=0)
            prob = jnp.exp2(dot(keys_long, qt[yq, :, cols]) * EXP_SCALE)
            if own:
                k_pos = lax.broadcasted_iota(jnp.int32, (BLK, QC), 0)
                q_pos = lax.broadcasted_iota(jnp.int32, (BLK, QC), 1) % BLK
                prob = jnp.where(k_pos <= q_pos, prob, 0.0)
            grad = prob * dot(values_long, gt[yq, :, cols])
            prob_half = prob.astype(BF16)
            grad_half = grad.astype(BF16)
            dv = dv + dot(prob_half, g_rows)
            dk = dk + dot(grad_half, q_rows)
            dqt[yq, :, cols] += dot(keys_t[dz, yk], grad_half)
        for c in range(2):
            acc[dz, c, yk, :, pl.ds(0, HDIM)] += dk[c * TOK : (c + 1) * TOK]
            acc[dz, c, yk, :, pl.ds(HDIM, HDIM)] += dv[c * TOK : (c + 1) * TOK]

    def dq_keep():
        return pltpu.make_async_copy(dq_half.at[y, core], dq_out.at[:, lanes(here, WIDE)], dq_local)

    def dq_give(column, c):
        return remote(
            dq_half.at[column, c], dq_out.at[:, lanes(here, WIDE)], dq_send.at[column, c], dq_recv.at[here],
            row + column * 2 + c,
        )

    def dq_take(p):
        remote(
            dq_half.at[0, 0], dq_out.at[:, lanes(p, WIDE)], dq_send.at[0, 0], dq_recv.at[p], sibling
        ).wait_recv()

    def finish_queries(column):
        for head in range(HEADS):
            done = (dqt[column, :, pl.ds(head * BLK, BLK)].T * SCALE).astype(BF16)
            for c in range(2):
                dq_half[column, c, :, pl.ds(head * HDIM, HDIM)] = done[c * TOK : (c + 1) * TOK]

        @pl.when(column == y)
        def _():
            dq_keep().start()
            dq_give(y, other).start()

        @pl.when(column != y)
        def _():
            for c in range(2):
                dq_give(column, c).start()

    def share(dz):
        return remote(acc.at[dz, other], xin.at[dz], s_send.at[dz], s_recv.at[dz], sibling)

    def along(dz):
        return remote(zout.at[2 - dz], zin.at[2 - dz], z_send.at[2 - dz], z_recv.at[2 - dz], down)

    def join(dz):
        share(dz).wait_recv()
        total = acc[dz, core] + xin[dz]
        acc[dz, core] = total

    def join_above(dz):
        remote(zout.at[1 - dz], zin.at[1 - dz], z_send.at[1 - dz], z_recv.at[1 - dz], down).wait_recv()
        acc[dz, core] += zin[1 - dz].astype(F32)

    def pass_down(dz):
        zout[2 - dz] = acc[dz, core].astype(SUMS)
        along(dz).start()

    @pl.loop(0, 12)
    def _(s):
        from1, from4, from8, from9, from10 = ((s + 12 - n) // 12 for n in (1, 4, 8, 9, 10))
        dz = from1 + from4 - from8 - from9
        turn = from1 * (s - 1) - 3 * from4 - from8 - from9 - 3 * from10
        yq = (y + turn + turn // 2 - 2 * (turn // 3)) % 4
        is0, is2 = (2 - dz) // 2, dz // 2
        live = (z - dz + 4) // 4
        first = is2 * yq
        last = 4 - is0 * (3 - yq)

        @pl.when((s == 1) & (z > 0))
        def _():
            kv_up(0).wait_recv()
            half(1).start()
            pl.when(z < 3)(lambda: kv_up(1).start())
            doc_up(0).wait_recv()
            pl.when(z < 3)(lambda: doc_up(1).start())
            half_take(1)

        @pl.when((s == 3) & (z > 1))
        def _():
            kv_up(1).wait_recv()
            half(2).start()
            doc_up(1).wait_recv()

        @pl.when((s == 4) & (z > 1))
        def _():
            half_take(2)

        pl.when(((s < 2) | (s == 4)) & (z >= dz))(lambda: prepare_keys(dz))

        @pl.when((s == 0) | (s == 2) | (s == 3) | (s == 7))
        def _():
            @pl.when(s == 0)
            def _():
                for kind in ("q", "g", "lse", "delta"):
                    stay(kind).wait()
                    receive(kind, others[0])

            @pl.when(s != 0)
            def _():
                for kind in ("q", "g", "lse", "delta"):
                    for c in range(2):
                        receive(kind, yq * 2 + c)

            @pl.when(s == 2)
            def _():
                for p in others[5:]:
                    for kind in ("q", "g", "lse", "delta"):
                        send(kind, p).start()

            prepare_queries(yq)

        @pl.loop(first, first + live * (last - first))
        def _(yk):
            diagonal = (dz == 0) & (yk == yq)
            pl.when(diagonal)(lambda: work(0, yq, yq, True))
            pl.when(jnp.logical_not(diagonal))(lambda: work(dz, yk, yq, False))

        @pl.when((s == 4) | (s >= 9))
        def _():
            finish_queries(yq)

        @pl.when((s == 7) & (z > 1))
        def _():
            share(2).start()

        @pl.when((s == 8) & (z > 0))
        def _():
            share(1).start()

            @pl.when(z > 1)
            def _():
                join(2)
                pass_down(2)

    share(0).start()

    @pl.when(z > 0)
    def _():
        join(1)
        pl.when(z < 3)(lambda: join_above(1))
        pass_down(1)

    join(0)
    pl.when(z < 3)(lambda: join_above(0))
    for column in range(4):
        fin[column, :, pl.ds(0, HDIM)] = (acc[0, core, column, :, pl.ds(0, HDIM)] * SCALE).astype(BF16)
        fin[column, :, pl.ds(HDIM, HDIM)] = acc[0, core, column, :, pl.ds(HDIM, HDIM)].astype(BF16)

    def fin_keep(part):
        return pltpu.make_async_copy(
            fin.at[y, :, pl.ds(part * HDIM, HDIM)], (dk_out, dv_out)[part].at[:, lanes(y, HDIM)], f_local.at[part]
        )

    def fin_give(part, column):
        return remote(
            fin.at[column, :, pl.ds(part * HDIM, HDIM)], (dk_out, dv_out)[part].at[:, lanes(y, HDIM)],
            f_send.at[part, column], f_recv.at[part, y], row + column * 2 + core,
        )

    def fin_take(part, column):
        remote(
            fin.at[column, :, pl.ds(part * HDIM, HDIM)], (dk_out, dv_out)[part].at[:, lanes(column, HDIM)],
            f_send.at[part, column], f_recv.at[part, column], sibling,
        ).wait_recv()

    for part in range(2):
        for column in columns:
            fin_give(part, column).start()
        fin_keep(part).start()

    for p in others:
        for kind in KINDS:
            send(kind, p).wait_send()
        dq_take(p)
    for dz in range(3):
        pl.when(z >= dz)(lambda dz=dz: half(dz).wait_send())
        pl.when(z >= dz)(lambda dz=dz: share(dz).wait_send())
    for dz in range(2):

        @pl.when((z >= dz) & (z < 3))
        def _():
            kv_up(dz).wait_send()
            doc_up(dz).wait_send()

    for dz in (1, 2):
        pl.when(z >= dz)(lambda dz=dz: along(dz).wait_send())
    dq_keep().wait()
    dq_give(y, other).wait_send()
    for column in columns:
        for c in range(2):
            dq_give(column, c).wait_send()
        for part in range(2):
            kv_give(part, column).wait_send()
            fin_give(part, column).wait_send()
            fin_take(part, column)
    for part in range(2):
        fin_keep(part).wait()


def on_device(queries, key_rows, value_rows, out_grad, log_norm, row_delta, doc_ids):
    dma = pltpu.SemaphoreType.DMA
    kinds = len(KINDS)
    dq, dk, dv = pl.pallas_call(
        kernel,
        out_shape=(
            jax.ShapeDtypeStruct((TOK, 8 * WIDE), BF16),
            jax.ShapeDtypeStruct((TOK, 4 * HDIM), BF16),
            jax.ShapeDtypeStruct((TOK, 4 * HDIM), BF16),
        ),
        in_specs=[pl.BlockSpec(memory_space=pl.ANY)] * 7,
        out_specs=[pl.BlockSpec(memory_space=pl.ANY)] * 3,
        scratch_shapes=[
            pltpu.VMEM((8, TOK, WIDE), BF16),
            pltpu.VMEM((8, TOK, WIDE), BF16),
            pltpu.VMEM((8, GROUP, TOK), F32),
            pltpu.VMEM((8, GROUP, TOK), F32),
            pltpu.VMEM((3, 8, 1, TOK), jnp.int32),
            pltpu.VMEM((3, 2, 4, TOK, 2 * HDIM), BF16),
            pltpu.VMEM((4, 2 * HDIM, COLS), BF16),
            pltpu.VMEM((4, 2 * HDIM, COLS), BF16),
            pltpu.VMEM((4, HDIM, COLS), F32),
            pltpu.VMEM((3, 4, BLK, HDIM), BF16),
            pltpu.VMEM((3, 4, HDIM, BLK), BF16),
            pltpu.VMEM((3, 2, 4, TOK, 2 * HDIM), F32),
            pltpu.VMEM((3, 4, TOK, 2 * HDIM), F32),
            pltpu.VMEM((2, 4, TOK, 2 * HDIM), SUMS),
            pltpu.VMEM((2, 4, TOK, 2 * HDIM), SUMS),
            pltpu.VMEM((4, 2, TOK, WIDE), BF16),
            pltpu.VMEM((4, TOK, 2 * HDIM), BF16),
            dma((kinds,)),
            dma((kinds, 8)),
            dma((kinds, 8)),
            dma((2,)),
            dma((2, 4)),
            dma((2, 4)),
            dma((3,)),
            dma((3,)),
            dma((2,)),
            dma((2,)),
            dma((2,)),
            dma((2,)),
            dma((3,)),
            dma((3,)),
            dma((2,)),
            dma((2,)),
            dma,
            dma((4, 2)),
            dma((8,)),
            dma((2,)),
            dma((2, 4)),
            dma((2, 4)),
        ],
        compiler_params=pltpu.CompilerParams(
            collective_id=0, has_side_effects=True, vmem_limit_bytes=60 * 2**20
        ),
        name="attention_backward",
    )(queries[0], key_rows[0], value_rows[0], out_grad[0], log_norm[0].T, row_delta[0].T, doc_ids)
    return dq[None], dk[None], dv[None]


def solution(mesh):
    return jax.shard_map(
        on_device,
        mesh=mesh,
        in_specs=(P("dp", "seq", None),) * 6 + (P("dp", "seq"),),
        out_specs=(P("dp", "seq", None),) * 3,
        check_vma=False,
    )
```

```python
import jax
import jax.numpy as jnp
from jax import lax
from jax.experimental import pallas as pl
from jax.experimental.pallas import tpu as pltpu
from jax.sharding import PartitionSpec as P

F32, BF16 = jnp.float32, jnp.bfloat16
HDIM = 128
TOK = 128
BLK = 2 * TOK
HEADS = 4
GROUP = 8
WIDE = HEADS * HDIM
COLS = HEADS * BLK
QC = 1024
SCALE = HDIM**-0.5
EXP_SCALE = SCALE * 1.4426950408889634
FAR = -1e30
MARKS = 16
KINDS = ("q", "g", "lse", "delta", "doc")
SUMS = BF16


def dot(a, b):
    return jnp.dot(a, b, preferred_element_type=F32)


def split3(x):
    hi = x.astype(BF16).astype(F32)
    mid = (x - hi).astype(BF16).astype(F32)
    return hi, mid, x - hi - mid


def kernel(
    q_in, k_in, v_in, g_in, lse_in, delta_in, doc_in,
    dq_out, dk_out, dv_out,
    q_buf, g_buf, lse_buf, delta_buf, doc_buf, kv, qt, gt, dqt, tails, keys_t, acc, xin, zout, zin, dq_half, fin,
    x_local, x_send, x_recv, kv_local, kv_send, kv_recv, half_send, half_recv, kvz_send, kvz_recv, docz_send, docz_recv,
    s_send, s_recv, z_send, z_recv, dq_local, dq_send, dq_recv, f_local, f_send, f_recv,
):
    me = lax.axis_index("seq")
    core = me % 2
    other = 1 - core
    y = (me // 2) % 4
    z = me // 8
    here = me % 8

    def remote(src, dst, send, recv, to):
        return pltpu.make_async_remote_copy(
            src_ref=src, dst_ref=dst, send_sem=send, recv_sem=recv,
            device_id={"seq": to}, device_id_type=pl.DeviceIdType.MESH,
        )

    row = z * 8
    sibling = row + y * 2 + other
    down, up = me - 8, me + 8

    def lanes(i, size):
        return pl.ds(pl.multiple_of(i * size, size), size)

    def source(kind, p):
        return {
            "q": lambda: q_in.at[:, lanes(p, WIDE)],
            "g": lambda: g_in.at[:, lanes(p, WIDE)],
            "lse": lambda: lse_in.at[lanes(p // 2, GROUP)],
            "delta": lambda: delta_in.at[lanes(p // 2, GROUP)],
            "doc": lambda: doc_in,
        }[kind]()

    def target(kind, p):
        return {
            "q": lambda: q_buf.at[p],
            "g": lambda: g_buf.at[p],
            "lse": lambda: lse_buf.at[p],
            "delta": lambda: delta_buf.at[p],
            "doc": lambda: doc_buf.at[0, p],
        }[kind]()

    def stay(kind):
        return pltpu.make_async_copy(source(kind, here), target(kind, here), x_local.at[KINDS.index(kind)])

    def send(kind, p):
        i = KINDS.index(kind)
        return remote(source(kind, p), target(kind, here), x_send.at[i, p], x_recv.at[i, here], row + p)

    def receive(kind, p):
        i = KINDS.index(kind)
        remote(source(kind, p), target(kind, p), x_send.at[i, p], x_recv.at[i, p], sibling).wait_recv()

    def kv_place(part, column):
        return kv.at[0, core, column, :, pl.ds(part * HDIM, HDIM)]

    def kv_source(part, column):
        return (k_in, v_in)[part].at[:, lanes(column, HDIM)]

    def kv_stay(part):
        return pltpu.make_async_copy(kv_source(part, y), kv_place(part, y), kv_local.at[part])

    def kv_give(part, column):
        return remote(
            kv_source(part, column), kv_place(part, y), kv_send.at[part, column], kv_recv.at[part, y],
            row + column * 2 + core,
        )

    def kv_take(part, column):
        remote(
            kv_source(part, column), kv_place(part, column), kv_send.at[part, column], kv_recv.at[part, column], sibling
        ).wait_recv()

    for part in range(2):
        kv_stay(part).start()
    for kind in KINDS:
        stay(kind).start()

    acc[...] = jnp.zeros_like(acc)
    barrier = pltpu.get_barrier_semaphore()

    def greet(to):
        pl.semaphore_signal(barrier, inc=1, device_id={"seq": to}, device_id_type=pl.DeviceIdType.MESH)

    for apart in range(1, 8):
        greet(row + (here + apart) % 8)
    pl.when(z > 0)(lambda: greet(down))
    pl.when(z < 3)(lambda: greet(up))
    pl.semaphore_wait(barrier, 7 + (z + 3) // 4 + (6 - z) // 4)

    columns = [(y + apart) % 4 for apart in (1, 3, 2)]
    others = [sibling - row] + [column * 2 + c for column in columns for c in range(2)]
    for column in columns:
        for part in range(2):
            kv_give(part, column).start()
    for p in others:
        send("doc", p).start()
    for p in others[:5]:
        for kind in ("q", "g", "lse", "delta"):
            send(kind, p).start()

    def half(dz):
        return remote(kv.at[dz, core], kv.at[dz, core], half_send.at[dz], half_recv.at[dz], sibling)

    def half_take(dz):
        remote(kv.at[dz, other], kv.at[dz, other], half_send.at[dz], half_recv.at[dz], sibling).wait_recv()

    def kv_up(dz, column):
        return remote(
            kv.at[dz, core, column], kv.at[dz + 1, core, column], kvz_send.at[dz, column], kvz_recv.at[dz, column], up
        )

    def doc_up(dz):
        return remote(doc_buf.at[dz], doc_buf.at[dz + 1], docz_send.at[dz], docz_recv.at[dz], up)

    for part in range(2):
        kv_stay(part).wait()
    pl.when(z < 3)(lambda: kv_up(0, y).start())
    for column in columns:
        for part in range(2):
            kv_take(part, column)
        pl.when(z < 3)(lambda column=column: kv_up(0, column).start())
    half(0).start()
    stay("doc").wait()
    for p in others:
        receive("doc", p)
    pl.when(z < 3)(lambda: doc_up(0).start())
    half_take(0)

    sixteen = lax.broadcasted_iota(jnp.int32, (MARKS, BLK), 0).astype(F32)

    def marks_of(dz, column):
        docs = jnp.concatenate([doc_buf[dz, column * 2], doc_buf[dz, column * 2 + 1]], axis=1).astype(F32)
        return jnp.broadcast_to(docs, (MARKS, BLK)) == sixteen

    def prepare_keys(dz):
        @pl.loop(0, 4)
        def _(column):
            marks = marks_of(dz, column).astype(F32)
            ones = (lax.broadcasted_iota(jnp.int32, (HDIM - MARKS, BLK), 0) < 6).astype(F32)
            tails[dz, column] = jnp.concatenate([marks, ones], axis=0).T.astype(BF16)
            keys_t[dz, column] = both(kv, dz, column, 0).T

    def both(ref, dz, column, part):
        at = pl.ds(part * HDIM, HDIM)
        return jnp.concatenate([ref[dz, 0, column, :, at], ref[dz, 1, column, :, at]], axis=0)

    def rows_of(buf, column, head):
        at = pl.ds(head * HDIM, HDIM)
        return jnp.concatenate([buf[column * 2, :, at], buf[column * 2 + 1, :, at]], axis=0)

    def prepare_queries(column):
        bias = jnp.where(marks_of(0, column), 0.0, FAR).astype(BF16)
        blank = jnp.zeros((MARKS, BLK), BF16)
        zeros = jnp.zeros((HDIM - 2 * MARKS, BLK), BF16)

        def statistic(buf, factor):
            pair = [buf[column * 2], buf[column * 2 + 1]]
            pair = [jnp.where(core == 0, rows[:HEADS], rows[HEADS:]) for rows in pair]
            return split3(jnp.concatenate(pair, axis=1) * factor)

        for buf, out, first, top, parts in (
            (q_buf, qt, 0, bias, statistic(lse_buf, -1.0 / SCALE)), (g_buf, gt, 3, blank, statistic(delta_buf, -1.0))
        ):
            for head in range(HEADS):
                at = pl.ds(head * BLK, BLK)
                rows = jnp.zeros((MARKS, BLK), F32)
                for i, part in enumerate(parts):
                    rows = jnp.where(sixteen == first + i, jnp.broadcast_to(part[head : head + 1], (MARKS, BLK)), rows)
                out[column, pl.ds(0, HDIM), at] = rows_of(buf, column, head).T
                out[column, pl.ds(HDIM, MARKS), at] = top
                out[column, pl.ds(HDIM + MARKS, MARKS), at] = rows.astype(BF16)
                out[column, pl.ds(HDIM + 2 * MARKS, HDIM - 2 * MARKS), at] = zeros
        dqt[column] = jnp.zeros((HDIM, COLS), F32)

    def work(dz, yks, yq, own=False):
        size = BLK * len(yks)

        def long(part):
            blocks = [jnp.concatenate([both(kv, dz, yk, part), tails[dz, yk]], axis=1) for yk in yks]
            return jnp.concatenate(blocks, axis=0)

        keys_long, values_long = long(0), long(1)
        across = jnp.concatenate([keys_t[dz, yk] for yk in yks], axis=1)
        dk = jnp.zeros((size, HDIM), F32)
        dv = jnp.zeros((size, HDIM), F32)
        for c in range(COLS // QC):
            cols = pl.ds(c * QC, QC)
            heads = [c * (QC // BLK) + i for i in range(QC // BLK)]
            q_rows = jnp.concatenate([rows_of(q_buf, yq, n) for n in heads], axis=0)
            g_rows = jnp.concatenate([rows_of(g_buf, yq, n) for n in heads], axis=0)
            prob = jnp.exp2(dot(keys_long, qt[yq, :, cols]) * EXP_SCALE)
            if own:
                k_pos = lax.broadcasted_iota(jnp.int32, (BLK, QC), 0)
                q_pos = lax.broadcasted_iota(jnp.int32, (BLK, QC), 1) % BLK
                prob = jnp.where(k_pos <= q_pos, prob, 0.0)
            grad = prob * dot(values_long, gt[yq, :, cols])
            prob_half = prob.astype(BF16)
            grad_half = grad.astype(BF16)
            dv = dv + dot(prob_half, g_rows)
            dk = dk + dot(grad_half, q_rows)
            dqt[yq, :, cols] += dot(across, grad_half)
        for i, yk in enumerate(yks):
            for c in range(2):
                at = slice(i * BLK + c * TOK, i * BLK + (c + 1) * TOK)
                acc[dz, c, yk, :, pl.ds(0, HDIM)] += dk[at]
                acc[dz, c, yk, :, pl.ds(HDIM, HDIM)] += dv[at]

    def dq_keep():
        return pltpu.make_async_copy(dq_half.at[y, core], dq_out.at[:, lanes(here, WIDE)], dq_local)

    def dq_give(column, c):
        return remote(
            dq_half.at[column, c], dq_out.at[:, lanes(here, WIDE)], dq_send.at[column, c], dq_recv.at[here],
            row + column * 2 + c,
        )

    def dq_take(p):
        remote(
            dq_half.at[0, 0], dq_out.at[:, lanes(p, WIDE)], dq_send.at[0, 0], dq_recv.at[p], sibling
        ).wait_recv()

    def finish_queries(column):
        for head in range(HEADS):
            done = (dqt[column, :, pl.ds(head * BLK, BLK)].T * SCALE).astype(BF16)
            for c in range(2):
                dq_half[column, c, :, pl.ds(head * HDIM, HDIM)] = done[c * TOK : (c + 1) * TOK]

        @pl.when(column == y)
        def _():
            dq_keep().start()
            dq_give(y, other).start()

        @pl.when(column != y)
        def _():
            for c in range(2):
                dq_give(column, c).start()

    def share(dz):
        return remote(acc.at[dz, other], xin.at[dz], s_send.at[dz], s_recv.at[dz], sibling)

    def along(dz, column):
        i = 2 - dz
        return remote(zout.at[i, column], zin.at[i, column], z_send.at[i, column], z_recv.at[i, column], down)

    def join(dz):
        share(dz).wait_recv()
        acc[dz, core] += xin[dz]

    def join_above(dz, column):
        i = 1 - dz
        remote(
            zout.at[i, column], zin.at[i, column], z_send.at[i, column], z_recv.at[i, column], down
        ).wait_recv()
        acc[dz, core, column] += zin[i, column].astype(F32)

    def pass_down(dz, column):
        zout[2 - dz, column] = acc[dz, core, column].astype(SUMS)
        along(dz, column).start()

    @pl.loop(0, 12)
    def _(s):
        from1, from4, from8, from9, from10 = ((s + 12 - n) // 12 for n in (1, 4, 8, 9, 10))
        dz = from1 + from4 - from8 - from9
        turn = from1 * (s - 1) - 3 * from4 - from8 - from9 - 3 * from10
        yq = (y + turn + turn // 2 - 2 * (turn // 3)) % 4
        is0, is2 = (2 - dz) // 2, dz // 2
        first = is2 * yq
        count = is0 * yq + is2 * (z // 2) * (4 - yq)

        @pl.when((s == 1) & (z > 0))
        def _():
            for column in [y] + columns:
                kv_up(0, column).wait_recv()
                pl.when(z < 3)(lambda column=column: kv_up(1, column).start())
            half(1).start()
            doc_up(0).wait_recv()
            pl.when(z < 3)(lambda: doc_up(1).start())
            half_take(1)

        @pl.when(s == 2)
        def _():
            for p in others[5:]:
                for kind in ("q", "g", "lse", "delta"):
                    send(kind, p).start()

        @pl.when((s == 3) & (z > 1))
        def _():
            for column in [y] + columns:
                kv_up(1, column).wait_recv()
            half(2).start()
            doc_up(1).wait_recv()

        @pl.when((s == 4) & (z > 1))
        def _():
            half_take(2)

        pl.when(((s < 2) | (s == 4)) & (z >= dz))(lambda: prepare_keys(dz))

        @pl.when((s == 0) | (s == 2) | (s == 3) | (s == 7))
        def _():
            @pl.when(s == 0)
            def _():
                for kind in ("q", "g", "lse", "delta"):
                    stay(kind).wait()
                    receive(kind, others[0])

            @pl.when(s != 0)
            def _():
                for kind in ("q", "g", "lse", "delta"):
                    for c in range(2):
                        receive(kind, yq * 2 + c)

            prepare_queries(yq)

        pl.when(dz == 0)(lambda: work(0, [yq], yq, True))
        pl.when((dz == 1) & (z > 0))(lambda: work(1, [0, 1, 2, 3], yq))

        @pl.loop(0, count // 2)
        def _(i):
            work(dz, [first + 2 * i, first + 2 * i + 1], yq)

        pl.when(count % 2 == 1)(lambda: work(dz, [first + count - 1], yq))

        @pl.when((s == 7) & (z > 1))
        def _():
            share(2).start()

        @pl.when((s == 8) & (z > 0))
        def _():
            share(1).start()

            @pl.when(z > 1)
            def _():
                join(2)
                for column in range(4):
                    pass_down(2, column)

        pl.when((s == 9) & (z > 0))(lambda: join(1))

        @pl.when((s == 10) & (z > 0))
        def _():
            @pl.loop(0, 4)
            def _(column):
                pl.when(z < 3)(lambda: join_above(1, column))
                pass_down(1, column)

        pl.when(s == 11)(lambda: share(0).start())

        @pl.when((s == 4) | (s >= 9))
        def _():
            finish_queries(yq)


    def fin_keep(part):
        return pltpu.make_async_copy(
            fin.at[y, :, pl.ds(part * HDIM, HDIM)], (dk_out, dv_out)[part].at[:, lanes(y, HDIM)], f_local.at[part]
        )

    def fin_give(part, column):
        return remote(
            fin.at[column, :, pl.ds(part * HDIM, HDIM)], (dk_out, dv_out)[part].at[:, lanes(y, HDIM)],
            f_send.at[part, column], f_recv.at[part, y], row + column * 2 + core,
        )

    def fin_take(part, column):
        remote(
            fin.at[column, :, pl.ds(part * HDIM, HDIM)], (dk_out, dv_out)[part].at[:, lanes(column, HDIM)],
            f_send.at[part, column], f_recv.at[part, column], sibling,
        ).wait_recv()

    join(0)

    @pl.loop(0, 4)
    def _(column):
        pl.when(z < 3)(lambda: join_above(0, column))
        fin[column, :, pl.ds(0, HDIM)] = (acc[0, core, column, :, pl.ds(0, HDIM)] * SCALE).astype(BF16)
        fin[column, :, pl.ds(HDIM, HDIM)] = acc[0, core, column, :, pl.ds(HDIM, HDIM)].astype(BF16)

        @pl.when(column != y)
        def _():
            for part in range(2):
                fin_give(part, column).start()

        @pl.when(column == y)
        def _():
            for part in range(2):
                fin_keep(part).start()

    for p in others:
        for kind in KINDS:
            send(kind, p).wait_send()
        dq_take(p)
    for dz in range(3):
        pl.when(z >= dz)(lambda dz=dz: half(dz).wait_send())
        pl.when(z >= dz)(lambda dz=dz: share(dz).wait_send())
    for dz in range(2):

        @pl.when((z >= dz) & (z < 3))
        def _():
            for column in range(4):
                kv_up(dz, column).wait_send()
            doc_up(dz).wait_send()

    for dz in (1, 2):
        for column in range(4):
            pl.when(z >= dz)(lambda dz=dz, column=column: along(dz, column).wait_send())
    dq_keep().wait()
    dq_give(y, other).wait_send()
    for column in columns:
        for c in range(2):
            dq_give(column, c).wait_send()
        for part in range(2):
            kv_give(part, column).wait_send()
            fin_give(part, column).wait_send()
            fin_take(part, column)
    for part in range(2):
        fin_keep(part).wait()


def on_device(queries, key_rows, value_rows, out_grad, log_norm, row_delta, doc_ids):
    dma = pltpu.SemaphoreType.DMA
    kinds = len(KINDS)
    dq, dk, dv = pl.pallas_call(
        kernel,
        out_shape=(
            jax.ShapeDtypeStruct((TOK, 8 * WIDE), BF16),
            jax.ShapeDtypeStruct((TOK, 4 * HDIM), BF16),
            jax.ShapeDtypeStruct((TOK, 4 * HDIM), BF16),
        ),
        in_specs=[pl.BlockSpec(memory_space=pl.ANY)] * 7,
        out_specs=[pl.BlockSpec(memory_space=pl.ANY)] * 3,
        scratch_shapes=[
            pltpu.VMEM((8, TOK, WIDE), BF16),
            pltpu.VMEM((8, TOK, WIDE), BF16),
            pltpu.VMEM((8, GROUP, TOK), F32),
            pltpu.VMEM((8, GROUP, TOK), F32),
            pltpu.VMEM((3, 8, 1, TOK), jnp.int32),
            pltpu.VMEM((3, 2, 4, TOK, 2 * HDIM), BF16),
            pltpu.VMEM((4, 2 * HDIM, COLS), BF16),
            pltpu.VMEM((4, 2 * HDIM, COLS), BF16),
            pltpu.VMEM((4, HDIM, COLS), F32),
            pltpu.VMEM((3, 4, BLK, HDIM), BF16),
            pltpu.VMEM((3, 4, HDIM, BLK), BF16),
            pltpu.VMEM((3, 2, 4, TOK, 2 * HDIM), F32),
            pltpu.VMEM((3, 4, TOK, 2 * HDIM), F32),
            pltpu.VMEM((2, 4, TOK, 2 * HDIM), SUMS),
            pltpu.VMEM((2, 4, TOK, 2 * HDIM), SUMS),
            pltpu.VMEM((4, 2, TOK, WIDE), BF16),
            pltpu.VMEM((4, TOK, 2 * HDIM), BF16),
            dma((kinds,)),
            dma((kinds, 8)),
            dma((kinds, 8)),
            dma((2,)),
            dma((2, 4)),
            dma((2, 4)),
            dma((3,)),
            dma((3,)),
            dma((2, 4)),
            dma((2, 4)),
            dma((2,)),
            dma((2,)),
            dma((3,)),
            dma((3,)),
            dma((2, 4)),
            dma((2, 4)),
            dma,
            dma((4, 2)),
            dma((8,)),
            dma((2,)),
            dma((2, 4)),
            dma((2, 4)),
        ],
        compiler_params=pltpu.CompilerParams(
            collective_id=0, has_side_effects=True, vmem_limit_bytes=60 * 2**20
        ),
        name="attention_backward",
    )(queries[0], key_rows[0], value_rows[0], out_grad[0], log_norm[0].T, row_delta[0].T, doc_ids)
    return dq[None], dk[None], dv[None]


def solution(mesh):
    return jax.shard_map(
        on_device,
        mesh=mesh,
        in_specs=(P("dp", "seq", None),) * 6 + (P("dp", "seq"),),
        out_specs=(P("dp", "seq", None),) * 3,
        check_vma=False,
    )
```

```python
import jax
import jax.numpy as jnp
from jax import lax
from jax.experimental import pallas as pl
from jax.experimental.pallas import tpu as pltpu
from jax.sharding import PartitionSpec as P

F32, BF16 = jnp.float32, jnp.bfloat16
HDIM = 128
TOK = 128
BLK = 2 * TOK
HEADS = 4
GROUP = 8
WIDE = HEADS * HDIM
COLS = HEADS * BLK
QC = 1024
SCALE = HDIM**-0.5
EXP_SCALE = SCALE * 1.4426950408889634
FAR = -1e30
MARKS = 16
KINDS = ("q", "g", "lse", "delta", "doc")
SUMS = BF16


def dot(a, b):
    return jnp.dot(a, b, preferred_element_type=F32)


def split3(x):
    hi = x.astype(BF16).astype(F32)
    mid = (x - hi).astype(BF16).astype(F32)
    return hi, mid, x - hi - mid


def kernel(
    q_in, k_in, v_in, g_in, lse_in, delta_in, doc_in,
    dq_out, dk_out, dv_out,
    q_buf, g_buf, lse_buf, delta_buf, doc_buf, kv, qt, gt, dqt, tails, keys_t, acc, xin, zout, zin, dq_half, fin,
    x_local, x_send, x_recv, kv_local, kv_send, kv_recv, half_send, half_recv, kvz_send, kvz_recv, docz_send, docz_recv,
    s_send, s_recv, z_send, z_recv, dq_local, dq_send, dq_recv, f_local, f_send, f_recv,
):
    me = lax.axis_index("seq")
    core = me % 2
    other = 1 - core
    y = (me // 2) % 4
    z = me // 8
    here = me % 8

    def remote(src, dst, send, recv, to):
        return pltpu.make_async_remote_copy(
            src_ref=src, dst_ref=dst, send_sem=send, recv_sem=recv,
            device_id={"seq": to}, device_id_type=pl.DeviceIdType.MESH,
        )

    row = z * 8
    sibling = row + y * 2 + other
    down, up = me - 8, me + 8

    def lanes(i, size):
        return pl.ds(pl.multiple_of(i * size, size), size)

    def source(kind, p):
        return {
            "q": lambda: q_in.at[:, lanes(p, WIDE)],
            "g": lambda: g_in.at[:, lanes(p, WIDE)],
            "lse": lambda: lse_in.at[lanes(p // 2, GROUP)],
            "delta": lambda: delta_in.at[lanes(p // 2, GROUP)],
            "doc": lambda: doc_in,
        }[kind]()

    def target(kind, p):
        return {
            "q": lambda: q_buf.at[p],
            "g": lambda: g_buf.at[p],
            "lse": lambda: lse_buf.at[p],
            "delta": lambda: delta_buf.at[p],
            "doc": lambda: doc_buf.at[0, p],
        }[kind]()

    def stay(kind):
        return pltpu.make_async_copy(source(kind, here), target(kind, here), x_local.at[KINDS.index(kind)])

    def send(kind, p):
        i = KINDS.index(kind)
        return remote(source(kind, p), target(kind, here), x_send.at[i, p], x_recv.at[i, here], row + p)

    def receive(kind, p):
        i = KINDS.index(kind)
        remote(source(kind, p), target(kind, p), x_send.at[i, p], x_recv.at[i, p], sibling).wait_recv()

    def kv_place(part, column):
        return kv.at[0, core, column, :, pl.ds(part * HDIM, HDIM)]

    def kv_source(part, column):
        return (k_in, v_in)[part].at[:, lanes(column, HDIM)]

    def kv_stay(part):
        return pltpu.make_async_copy(kv_source(part, y), kv_place(part, y), kv_local.at[part])

    def kv_give(part, column):
        return remote(
            kv_source(part, column), kv_place(part, y), kv_send.at[part, column], kv_recv.at[part, y],
            row + column * 2 + core,
        )

    def kv_take(part, column):
        remote(
            kv_source(part, column), kv_place(part, column), kv_send.at[part, column], kv_recv.at[part, column], sibling
        ).wait_recv()

    for part in range(2):
        kv_stay(part).start()
    for kind in KINDS:
        stay(kind).start()

    acc[...] = jnp.zeros_like(acc)
    barrier = pltpu.get_barrier_semaphore()

    def greet(to):
        pl.semaphore_signal(barrier, inc=1, device_id={"seq": to}, device_id_type=pl.DeviceIdType.MESH)

    for apart in range(1, 8):
        greet(row + (here + apart) % 8)
    pl.when(z > 0)(lambda: greet(down))
    pl.when(z < 3)(lambda: greet(up))
    pl.semaphore_wait(barrier, 7 + (z + 3) // 4 + (6 - z) // 4)

    columns = [(y + apart) % 4 for apart in (1, 3, 2)]
    others = [sibling - row] + [column * 2 + c for column in columns for c in range(2)]
    for column in columns:
        for part in range(2):
            kv_give(part, column).start()
    for p in others:
        send("doc", p).start()
    for p in others[:5]:
        for kind in ("q", "g", "lse", "delta"):
            send(kind, p).start()

    def half(dz):
        return remote(kv.at[dz, core], kv.at[dz, core], half_send.at[dz], half_recv.at[dz], sibling)

    def half_take(dz):
        remote(kv.at[dz, other], kv.at[dz, other], half_send.at[dz], half_recv.at[dz], sibling).wait_recv()

    def kv_up(dz, column):
        return remote(
            kv.at[dz, core, column], kv.at[dz + 1, core, column], kvz_send.at[dz, column], kvz_recv.at[dz, column], up
        )

    def doc_up(dz):
        return remote(doc_buf.at[dz], doc_buf.at[dz + 1], docz_send.at[dz], docz_recv.at[dz], up)

    for part in range(2):
        kv_stay(part).wait()
    pl.when(z < 3)(lambda: kv_up(0, y).start())
    for column in columns:
        for part in range(2):
            kv_take(part, column)
        pl.when(z < 3)(lambda column=column: kv_up(0, column).start())
    half(0).start()
    stay("doc").wait()
    for p in others:
        receive("doc", p)
    pl.when(z < 3)(lambda: doc_up(0).start())
    half_take(0)

    sixteen = lax.broadcasted_iota(jnp.int32, (MARKS, BLK), 0).astype(F32)

    def marks_of(dz, column):
        docs = jnp.concatenate([doc_buf[dz, column * 2], doc_buf[dz, column * 2 + 1]], axis=1).astype(F32)
        return jnp.broadcast_to(docs, (MARKS, BLK)) == sixteen

    def prepare_keys(dz):
        @pl.loop(0, 4)
        def _(column):
            marks = marks_of(dz, column).astype(F32)
            ones = (lax.broadcasted_iota(jnp.int32, (HDIM - MARKS, BLK), 0) < 6).astype(F32)
            tails[dz, column] = jnp.concatenate([marks, ones], axis=0).T.astype(BF16)
            keys_t[dz, column] = both(kv, dz, column, 0).T

    def both(ref, dz, column, part):
        at = pl.ds(part * HDIM, HDIM)
        return jnp.concatenate([ref[dz, 0, column, :, at], ref[dz, 1, column, :, at]], axis=0)

    def rows_of(buf, column, head):
        at = pl.ds(head * HDIM, HDIM)
        return jnp.concatenate([buf[column * 2, :, at], buf[column * 2 + 1, :, at]], axis=0)

    def prepare_queries(column):
        bias = jnp.where(marks_of(0, column), 0.0, FAR).astype(BF16)
        blank = jnp.zeros((MARKS, BLK), BF16)
        zeros = jnp.zeros((HDIM - 2 * MARKS, BLK), BF16)

        def statistic(buf, factor):
            pair = [buf[column * 2], buf[column * 2 + 1]]
            pair = [jnp.where(core == 0, rows[:HEADS], rows[HEADS:]) for rows in pair]
            return split3(jnp.concatenate(pair, axis=1) * factor)

        for buf, out, first, top, parts in (
            (q_buf, qt, 0, bias, statistic(lse_buf, -1.0 / SCALE)), (g_buf, gt, 3, blank, statistic(delta_buf, -1.0))
        ):
            for head in range(HEADS):
                at = pl.ds(head * BLK, BLK)
                rows = jnp.zeros((MARKS, BLK), F32)
                for i, part in enumerate(parts):
                    rows = jnp.where(sixteen == first + i, jnp.broadcast_to(part[head : head + 1], (MARKS, BLK)), rows)
                out[column, pl.ds(0, HDIM), at] = rows_of(buf, column, head).T
                out[column, pl.ds(HDIM, MARKS), at] = top
                out[column, pl.ds(HDIM + MARKS, MARKS), at] = rows.astype(BF16)
                out[column, pl.ds(HDIM + 2 * MARKS, HDIM - 2 * MARKS), at] = zeros
        dqt[column] = jnp.zeros((HDIM, COLS), F32)

    def work(dz, yks, yq, own=False):
        size = BLK * len(yks)

        def long(part):
            blocks = [jnp.concatenate([both(kv, dz, yk, part), tails[dz, yk]], axis=1) for yk in yks]
            return jnp.concatenate(blocks, axis=0)

        keys_long, values_long = long(0), long(1)
        across = jnp.concatenate([keys_t[dz, yk] for yk in yks], axis=1)
        dk = jnp.zeros((size, HDIM), F32)
        dv = jnp.zeros((size, HDIM), F32)
        for c in range(COLS // QC):
            cols = pl.ds(c * QC, QC)
            heads = [c * (QC // BLK) + i for i in range(QC // BLK)]
            q_rows = jnp.concatenate([rows_of(q_buf, yq, n) for n in heads], axis=0)
            g_rows = jnp.concatenate([rows_of(g_buf, yq, n) for n in heads], axis=0)
            prob = jnp.exp2(dot(keys_long, qt[yq, :, cols]) * EXP_SCALE)
            if own:
                k_pos = lax.broadcasted_iota(jnp.int32, (BLK, QC), 0)
                q_pos = lax.broadcasted_iota(jnp.int32, (BLK, QC), 1) % BLK
                prob = jnp.where(k_pos <= q_pos, prob, 0.0)
            grad = prob * dot(values_long, gt[yq, :, cols])
            prob_half = prob.astype(BF16)
            grad_half = grad.astype(BF16)
            dv = dv + dot(prob_half, g_rows)
            dk = dk + dot(grad_half, q_rows)
            dqt[yq, :, cols] += dot(across, grad_half)
        for i, yk in enumerate(yks):
            for c in range(2):
                at = slice(i * BLK + c * TOK, i * BLK + (c + 1) * TOK)
                acc[dz, c, yk, :, pl.ds(0, HDIM)] += dk[at]
                acc[dz, c, yk, :, pl.ds(HDIM, HDIM)] += dv[at]

    def dq_keep():
        return pltpu.make_async_copy(dq_half.at[y, core], dq_out.at[:, lanes(here, WIDE)], dq_local)

    def dq_give(column, c):
        return remote(
            dq_half.at[column, c], dq_out.at[:, lanes(here, WIDE)], dq_send.at[column, c], dq_recv.at[here],
            row + column * 2 + c,
        )

    def dq_take(p):
        remote(
            dq_half.at[0, 0], dq_out.at[:, lanes(p, WIDE)], dq_send.at[0, 0], dq_recv.at[p], sibling
        ).wait_recv()

    def finish_queries(column):
        for head in range(HEADS):
            done = (dqt[column, :, pl.ds(head * BLK, BLK)].T * SCALE).astype(BF16)
            for c in range(2):
                dq_half[column, c, :, pl.ds(head * HDIM, HDIM)] = done[c * TOK : (c + 1) * TOK]

        @pl.when(column == y)
        def _():
            dq_keep().start()
            dq_give(y, other).start()

        @pl.when(column != y)
        def _():
            for c in range(2):
                dq_give(column, c).start()

    def share(dz):
        return remote(acc.at[dz, other], xin.at[dz], s_send.at[dz], s_recv.at[dz], sibling)

    def along(dz, column):
        i = 2 - dz
        return remote(zout.at[i, column], zin.at[i, column], z_send.at[i, column], z_recv.at[i, column], down)

    def join(dz):
        share(dz).wait_recv()
        acc[dz, core] += xin[dz]

    def join_above(dz, column):
        i = 1 - dz
        remote(
            zout.at[i, column], zin.at[i, column], z_send.at[i, column], z_recv.at[i, column], down
        ).wait_recv()
        acc[dz, core, column] += zin[i, column].astype(F32)

    def pass_down(dz, column):
        zout[2 - dz, column] = acc[dz, core, column].astype(SUMS)
        along(dz, column).start()

    @pl.loop(0, 12)
    def _(s):
        from1, from4, from7, from8, from9, from10, from11 = ((s + 12 - n) // 12 for n in (1, 4, 7, 8, 9, 10, 11))
        dz = from1 + from4 - 2 * from7 + 2 * from8 - 2 * from9 + from10 - from11
        turn = from1 * (s - 1) - 3 * from4 - 2 * from7 + from8 - from9 - from10 - 2 * from11
        yq = (y + turn + turn // 2 - 2 * (turn // 3)) % 4
        is0, is2 = (2 - dz) // 2, dz // 2
        first = is2 * yq
        count = is0 * yq + is2 * (z // 2) * (4 - yq)

        @pl.when((s == 1) & (z > 0))
        def _():
            for column in [y] + columns:
                kv_up(0, column).wait_recv()
                pl.when(z < 3)(lambda column=column: kv_up(1, column).start())
            half(1).start()
            doc_up(0).wait_recv()
            pl.when(z < 3)(lambda: doc_up(1).start())
            half_take(1)

        @pl.when(s == 2)
        def _():
            for p in others[5:]:
                for kind in ("q", "g", "lse", "delta"):
                    send(kind, p).start()

        @pl.when((s == 3) & (z > 1))
        def _():
            for column in [y] + columns:
                kv_up(1, column).wait_recv()
            half(2).start()
            doc_up(1).wait_recv()

        @pl.when((s == 4) & (z > 1))
        def _():
            half_take(2)

        pl.when(((s < 2) | (s == 4)) & (z >= dz))(lambda: prepare_keys(dz))

        @pl.when((s == 0) | (s == 2) | (s == 3) | (s == 8))
        def _():
            @pl.when(s == 0)
            def _():
                for kind in ("q", "g", "lse", "delta"):
                    stay(kind).wait()
                    receive(kind, others[0])

            @pl.when(s != 0)
            def _():
                for kind in ("q", "g", "lse", "delta"):
                    for c in range(2):
                        receive(kind, yq * 2 + c)

            prepare_queries(yq)

        pl.when(dz == 0)(lambda: work(0, [yq], yq, True))
        pl.when((dz == 1) & (z > 0))(lambda: work(1, [0, 1, 2, 3], yq))

        @pl.loop(0, count // 2)
        def _(i):
            work(dz, [first + 2 * i, first + 2 * i + 1], yq)

        pl.when(count % 2 == 1)(lambda: work(dz, [first + count - 1], yq))

        @pl.when((s == 8) & (z > 1))
        def _():
            share(2).start()

        pl.when((s == 10) & (z > 0))(lambda: share(1).start())

        @pl.when((s == 9) & (z > 1))
        def _():
            join(2)
            for column in range(4):
                pass_down(2, column)

        pl.when((s == 11) & (z > 0))(lambda: join(1))

        pl.when(s == 11)(lambda: share(0).start())

        @pl.when((s == 4) | (s == 7) | (s >= 10))
        def _():
            finish_queries(yq)

        @pl.when((s == 11) & (z > 0))
        def _():
            @pl.loop(0, 4)
            def _(column):
                pl.when(z < 3)(lambda: join_above(1, column))
                pass_down(1, column)


    def fin_keep(part):
        return pltpu.make_async_copy(
            fin.at[y, :, pl.ds(part * HDIM, HDIM)], (dk_out, dv_out)[part].at[:, lanes(y, HDIM)], f_local.at[part]
        )

    def fin_give(part, column):
        return remote(
            fin.at[column, :, pl.ds(part * HDIM, HDIM)], (dk_out, dv_out)[part].at[:, lanes(y, HDIM)],
            f_send.at[part, column], f_recv.at[part, y], row + column * 2 + core,
        )

    def fin_take(part, column):
        remote(
            fin.at[column, :, pl.ds(part * HDIM, HDIM)], (dk_out, dv_out)[part].at[:, lanes(column, HDIM)],
            f_send.at[part, column], f_recv.at[part, column], sibling,
        ).wait_recv()

    join(0)

    @pl.loop(0, 4)
    def _(column):
        pl.when(z < 3)(lambda: join_above(0, column))
        fin[column, :, pl.ds(0, HDIM)] = (acc[0, core, column, :, pl.ds(0, HDIM)] * SCALE).astype(BF16)
        fin[column, :, pl.ds(HDIM, HDIM)] = acc[0, core, column, :, pl.ds(HDIM, HDIM)].astype(BF16)

        @pl.when(column != y)
        def _():
            for part in range(2):
                fin_give(part, column).start()

        @pl.when(column == y)
        def _():
            for part in range(2):
                fin_keep(part).start()

    for p in others:
        for kind in KINDS:
            send(kind, p).wait_send()
        dq_take(p)
    for dz in range(3):
        pl.when(z >= dz)(lambda dz=dz: half(dz).wait_send())
        pl.when(z >= dz)(lambda dz=dz: share(dz).wait_send())
    for dz in range(2):

        @pl.when((z >= dz) & (z < 3))
        def _():
            for column in range(4):
                kv_up(dz, column).wait_send()
            doc_up(dz).wait_send()

    for dz in (1, 2):
        for column in range(4):
            pl.when(z >= dz)(lambda dz=dz, column=column: along(dz, column).wait_send())
    dq_keep().wait()
    dq_give(y, other).wait_send()
    for column in columns:
        for c in range(2):
            dq_give(column, c).wait_send()
        for part in range(2):
            kv_give(part, column).wait_send()
            fin_give(part, column).wait_send()
            fin_take(part, column)
    for part in range(2):
        fin_keep(part).wait()


def on_device(queries, key_rows, value_rows, out_grad, log_norm, row_delta, doc_ids):
    dma = pltpu.SemaphoreType.DMA
    kinds = len(KINDS)
    dq, dk, dv = pl.pallas_call(
        kernel,
        out_shape=(
            jax.ShapeDtypeStruct((TOK, 8 * WIDE), BF16),
            jax.ShapeDtypeStruct((TOK, 4 * HDIM), BF16),
            jax.ShapeDtypeStruct((TOK, 4 * HDIM), BF16),
        ),
        in_specs=[pl.BlockSpec(memory_space=pl.ANY)] * 7,
        out_specs=[pl.BlockSpec(memory_space=pl.ANY)] * 3,
        scratch_shapes=[
            pltpu.VMEM((8, TOK, WIDE), BF16),
            pltpu.VMEM((8, TOK, WIDE), BF16),
            pltpu.VMEM((8, GROUP, TOK), F32),
            pltpu.VMEM((8, GROUP, TOK), F32),
            pltpu.VMEM((3, 8, 1, TOK), jnp.int32),
            pltpu.VMEM((3, 2, 4, TOK, 2 * HDIM), BF16),
            pltpu.VMEM((4, 2 * HDIM, COLS), BF16),
            pltpu.VMEM((4, 2 * HDIM, COLS), BF16),
            pltpu.VMEM((4, HDIM, COLS), F32),
            pltpu.VMEM((3, 4, BLK, HDIM), BF16),
            pltpu.VMEM((3, 4, HDIM, BLK), BF16),
            pltpu.VMEM((3, 2, 4, TOK, 2 * HDIM), F32),
            pltpu.VMEM((3, 4, TOK, 2 * HDIM), F32),
            pltpu.VMEM((2, 4, TOK, 2 * HDIM), SUMS),
            pltpu.VMEM((2, 4, TOK, 2 * HDIM), SUMS),
            pltpu.VMEM((4, 2, TOK, WIDE), BF16),
            pltpu.VMEM((4, TOK, 2 * HDIM), BF16),
            dma((kinds,)),
            dma((kinds, 8)),
            dma((kinds, 8)),
            dma((2,)),
            dma((2, 4)),
            dma((2, 4)),
            dma((3,)),
            dma((3,)),
            dma((2, 4)),
            dma((2, 4)),
            dma((2,)),
            dma((2,)),
            dma((3,)),
            dma((3,)),
            dma((2, 4)),
            dma((2, 4)),
            dma,
            dma((4, 2)),
            dma((8,)),
            dma((2,)),
            dma((2, 4)),
            dma((2, 4)),
        ],
        compiler_params=pltpu.CompilerParams(
            collective_id=0, has_side_effects=True, vmem_limit_bytes=60 * 2**20
        ),
        name="attention_backward",
    )(queries[0], key_rows[0], value_rows[0], out_grad[0], log_norm[0].T, row_delta[0].T, doc_ids)
    return dq[None], dk[None], dv[None]


def solution(mesh):
    return jax.shard_map(
        on_device,
        mesh=mesh,
        in_specs=(P("dp", "seq", None),) * 6 + (P("dp", "seq"),),
        out_specs=(P("dp", "seq", None),) * 3,
        check_vma=False,
    )
```
